1024 devices in a mesh: dp: 2 (over core), expert: 64 (over x_lo, z), tensor: 8 (over y, x_hi).
Axes of the slice: x: 4 (x_hi: 2, x_lo: 2; x = x_hi * 2 + x_lo), y: 4, z: 32, core: 2. Of those that a mesh axis runs over, the one named last changes fastest.
Arguments:
- residual: bfloat16 [16384, 4096], P(('dp', 'expert'), 'tensor'), may hold values from -6 to 6
- route_ids: int32 [16384, 2], P(('dp', 'expert')), may hold values from 0 to 63, all different within a row
- slot_hidden: bfloat16 [32768, 2560], P(('dp', 'expert')), may hold values from -6 to 6
- slot_gates: float32 [32768], P(('dp', 'expert')), may hold values from 0.1 to 1
- down_weight: bfloat16 [64, 2560, 4096], P('expert', None, 'tensor'), may hold values from -0.125 to 0.125
- cotangent: bfloat16 [16384, 4096], P(('dp', 'expert'), 'tensor'), may hold values from -3 to 3
Outputs:
- combined: bfloat16 [16384, 4096], P(('dp', 'expert'), 'tensor')
- hidden_grad: bfloat16 [32768, 2560], P(('dp', 'expert'), 'tensor')
- gate_grad: float32 [32768], P(('dp', 'expert', 'tensor'))
- down_weight_gradient: bfloat16 [64, 2560, 4096], P('expert', 'dp', 'tensor')
The draws below stay inside these ranges and needn't reach their ends.
Inputs may be any that keep to these rules, and one draw needn't show every extreme that they name: `route_ids`: the two experts of a token differ.
All inputs are finite; a program needn't handle non-finite values.
Results may differ from the reference program's by a relative error of at most 0.022.
Values may be sent and summed in bfloat16 or wider, within the bound.
No kernel may reach another device: no remote copies, remote signals or barrier semaphores. Data moves between devices by JAX's collectives and lax.ppermute only.
A program may use at most 64 MiB of HBM per device.

```python
import jax
import jax.numpy as jnp
from jax import lax

D = 4096
FF = 2560
TOK_DEV = 128
EXPERTS = 64
C_SRC = 4
CAP = 256
TOKENS = 16384
N_DP = 2
N_EXPERT = 64
N_TENSOR = 8


def level_of(rng, shape, shards, low, top_value):
    def one(position, shards_of):
        steps = jax.random.uniform(jax.random.fold_in(jax.random.fold_in(rng, 6), position), (shards_of,), jnp.float32, low / len(shards), top_value / len(shards))
        return jnp.repeat(jnp.exp(steps), shape[position] // shards_of).reshape((-1,) + (1,) * (len(shape) - position - 1))

    loudness = one(*shards[0])
    for cut in shards[1:]:
        loudness = loudness * one(*cut)
    return loudness


def distinct(own_key, rows, amount, top, lift):
    ranking = jax.random.permutation(jax.random.fold_in(own_key, 1), amount)
    favour = ranking
    for power in range(3):
        favour = favour * favour // amount
    favour = favour * lift // amount
    chance = jax.random.randint(jax.random.fold_in(own_key, 2), (rows, amount), 0, 4096) + favour
    sure = jax.random.permutation(jax.random.fold_in(own_key, 3), rows)[jnp.arange(amount) % rows]
    chance = jnp.where(jnp.arange(rows)[:, None] == sure[None, :], 1 << 14, chance)
    merit = chance * amount + jnp.arange(amount)
    return lax.top_k(merit.astype(jnp.int32), top)[1].astype(jnp.int32)


def gaussian(key, dims, width, reach, cuts=(), kind=jnp.bfloat16):
    values = width * jax.random.normal(key, dims, jnp.float32)
    if cuts:
        values = values * level_of(key, dims, cuts, -0.22, 0.18)
    return jnp.clip(values, -reach, reach).astype(kind)


def setup_inputs(seed: int = 0) -> dict:
    streams_of = jax.random.split(jax.random.key(seed), 7)
    return {
        "residual": gaussian(streams_of[0], (TOKENS, D), 1.0, 6.0, ((0, 128), (1, 8))),
        "route_ids": distinct(streams_of[1], TOKENS, EXPERTS, 2, 512),
        "slot_hidden": gaussian(streams_of[2], (N_DP * EXPERTS * CAP, FF), 1.0, 6.0, ((0, 128),)),
        "slot_gates": jnp.clip(0.1 + 0.9 * jax.random.uniform(streams_of[3], (N_DP * EXPERTS * CAP,), jnp.float32) ** level_of(streams_of[3], (N_DP * EXPERTS * CAP,), ((0, 128),), -0.2, 0.2), 0.1, 1.0),
        "down_weight": gaussian(streams_of[4], (EXPERTS, FF, D), FF ** -0.5, 0.125, ((0, 64), (2, 8))),
        "cotangent": gaussian(streams_of[5], (TOKENS, D), 0.5, 3.0, ((0, 128), (1, 8))),
    }


def reference(residual, route_ids, slot_hidden, slot_gates, down_weight, cotangent):
    groups = N_DP * N_EXPERT
    total = N_DP * EXPERTS * CAP
    width_block = D // N_TENSOR
    picks = route_ids.reshape(groups, TOK_DEV * 2).astype(jnp.int32)
    expert_iota = jnp.arange(EXPERTS, dtype=jnp.int32)
    onehot = (picks[:, :, None] == expert_iota[None, None, :]).astype(jnp.int32)
    before = jnp.cumsum(onehot, axis=1) - onehot
    rank_of = jnp.sum(before * onehot, axis=2).astype(jnp.int32)
    kept = rank_of < C_SRC
    group_iota = jnp.arange(groups, dtype=jnp.int32)
    source = group_iota % N_EXPERT
    data_group = group_iota // N_EXPERT
    rows = (data_group[:, None] * EXPERTS + picks) * CAP + source[:, None] * C_SRC + rank_of
    rows = jnp.where(kept, rows, total).reshape(-1).astype(jnp.int32)
    kept_flat = kept.reshape(-1)
    repeated = jnp.repeat(cotangent, 2, axis=0)
    slot_cot = jnp.zeros((total, D), jnp.bfloat16).at[rows].set(repeated, mode="drop")

    hidden_four = jnp.moveaxis(slot_hidden.reshape(N_DP, EXPERTS, CAP, FF), 1, 0)
    gates_three = jnp.moveaxis(slot_gates.reshape(N_DP, EXPERTS, CAP), 1, 0)
    cotangent_four = jnp.moveaxis(slot_cot.reshape(N_DP, EXPERTS, CAP, D), 1, 0)

    def one_expert(items):
        hidden, gates, slot_grad, weight = items
        hidden = hidden.reshape(N_DP * CAP, FF)
        gates = gates.reshape(N_DP * CAP, 1).astype(jnp.float32)
        slot_grad = slot_grad.reshape(N_DP * CAP, D).astype(jnp.float32)
        projected = jnp.dot(hidden, weight, preferred_element_type=jnp.float32)
        slot_out = (gates * projected).astype(jnp.bfloat16)
        scaled = (gates * slot_grad).astype(jnp.bfloat16)
        down_weight_gradient = jnp.dot(hidden.T, scaled, preferred_element_type=jnp.float32).astype(jnp.bfloat16)
        block_scaled_values = scaled.astype(jnp.float32).reshape(N_DP * CAP, N_TENSOR, width_block)
        block_weight_tiles = weight.astype(jnp.float32).reshape(FF, N_TENSOR, width_block)
        addend_terms = jnp.einsum("akh,qkh->kaq", block_scaled_values, block_weight_tiles)
        addend_terms = lax.optimization_barrier(addend_terms.astype(jnp.bfloat16)).astype(jnp.float32)
        hidden_grad = jnp.sum(addend_terms, axis=0).astype(jnp.bfloat16)
        gate_terms = jnp.sum((slot_grad * projected).reshape(N_DP * CAP, N_TENSOR, width_block), axis=2)
        gate_terms = lax.optimization_barrier(gate_terms.astype(jnp.bfloat16)).astype(jnp.float32)
        gate_grad = jnp.sum(gate_terms, axis=1)
        return (slot_out.reshape(N_DP, CAP, D), hidden_grad.reshape(N_DP, CAP, FF),
                gate_grad.reshape(N_DP, CAP), down_weight_gradient)

    slot_out, hidden_grad, gate_grad, down_weight_gradient = lax.map(
        one_expert, (hidden_four, gates_three, cotangent_four, down_weight))
    slot_out = jnp.moveaxis(slot_out, 0, 1).reshape(total, D)
    hidden_grad = jnp.moveaxis(hidden_grad, 0, 1).reshape(total, FF)
    gate_grad = jnp.moveaxis(gate_grad, 0, 1).reshape(total)

    safe_rows = jnp.where(kept_flat, rows, 0).astype(jnp.int32)
    picked = slot_out[safe_rows].astype(jnp.float32) * kept_flat[:, None].astype(jnp.float32)
    reduced_total = jnp.sum(picked.reshape(TOKENS, 2, D), axis=1)
    combined = (residual.astype(jnp.float32) + reduced_total).astype(jnp.bfloat16)
    return (combined, hidden_grad, gate_grad, down_weight_gradient)
```

```python
import jax
import jax.numpy as jnp
from jax import lax
from jax.experimental import pallas as pl
from jax.experimental.pallas import tpu as pltpu
from jax.sharding import PartitionSpec as P

F32 = jnp.float32
BF16 = jnp.bfloat16
EXTRA = 16


def iota(shape, dim):
    return lax.broadcasted_iota(jnp.int32, shape, dim)


def column_of(row):
    n = row.shape[1]
    same = iota((n, n), 0) == iota((n, n), 1)
    return jnp.sum(jnp.where(same, jnp.broadcast_to(row, (n, n)), 0.0), axis=1, keepdims=True)


def route_hits(ids, experts, per):
    tokens = ids.shape[1]
    rows = experts * 2 * per
    slot = iota((rows, tokens), 0)
    owner = slot // (2 * per)
    place = slot % (2 * per)
    named = jnp.logical_or(ids[0:1, :] == owner, ids[1:2, :] == owner)
    earlier = (iota((tokens, tokens), 0) < iota((tokens, tokens), 1)).astype(F32).astype(BF16)
    rank = jnp.dot(named.astype(F32).astype(BF16), earlier, preferred_element_type=F32).astype(jnp.int32)
    send = jnp.logical_and(named, rank == place)
    send = jnp.logical_and(send, place < per)
    take = jnp.logical_and(named, rank + per == place)
    return send.astype(F32).astype(BF16), take.astype(F32).astype(BF16)


def spread(slots, per, offset):
    row, slot = iota((2 * slots, slots), 0), iota((2 * slots, slots), 1)
    return ((slot // per) * 2 * per + offset + slot % per == row).astype(F32).astype(BF16)


def send_kernel(experts, per, ids, cotangent, hidden, weight, gates, message, take, projected):
    gate = column_of(gates[...])
    product = jnp.dot(hidden[...], weight[...], preferred_element_type=F32)
    projected[...] = product
    outgoing = (gate * product).astype(BF16)
    send_hits, take_hits = route_hits(ids[...], experts, per)
    take[...] = take_hits
    slots = experts * per
    rows = jnp.dot(send_hits, cotangent[...], preferred_element_type=F32)
    rows += jnp.dot(spread(slots, per, per), outgoing, preferred_element_type=F32)
    message[...] = rows.astype(BF16)


def hidden_kernel(experts, per, parts, arrived, weight, gates, projected, scaled, partial):
    slots = experts * per
    gate = column_of(gates[...])
    slot_grad = lax.dot_general(
        spread(slots, per, 0), arrived[...], (((0,), (0,)), ((), ())), preferred_element_type=F32
    )
    grown = (gate * slot_grad).astype(BF16)
    scaled[...] = grown
    terms = jnp.sum(slot_grad * projected[...], axis=1, keepdims=True).astype(BF16).astype(F32)
    width = slots // parts
    chosen = (iota((parts, slots), 1) // width == iota((parts, slots), 0)).astype(F32).astype(BF16)
    lanes = jnp.where(iota((slots, slots), 0) % width == iota((slots, slots), 1), terms, 0.0).astype(BF16)
    gate_rows = jnp.dot(chosen, lanes, preferred_element_type=F32)
    block = weight.shape[0] // parts
    for part in range(parts):
        partial[part, :block, :] = lax.dot_general(
            weight[part * block : (part + 1) * block, :], grown, (((1,), (1,)), ((), ())),
            preferred_element_type=F32,
        ).astype(BF16)
        tail = jnp.where(iota((EXTRA, slots), 0) == 0, gate_rows[part : part + 1, :], 0.0)
        partial[part, block:, :] = tail.astype(BF16)


def weight_kernel(hidden, scaled, out):
    step = 512
    for begin in range(0, hidden.shape[1], step):
        out[begin : begin + step, :] = lax.dot_general(
            hidden[:, begin : begin + step], scaled[...], (((0,), (0,)), ((), ())), preferred_element_type=F32
        ).astype(BF16)


def combine_kernel(arrived, take, residual, out):
    reduced = lax.dot_general(take[...], arrived[...], (((0,), (0,)), ((), ())), preferred_element_type=F32)
    out[...] = (residual[...].astype(F32) + reduced).astype(BF16)


def sum_kernel(parts, partial, hidden_grad, gate_grad):
    block, width = hidden_grad.shape[0], gate_grad.shape[1]
    total = partial[0, :block, :].astype(F32)
    gate = partial[0, block:, :].astype(F32)
    for part in range(1, parts):
        total += partial[part, :block, :].astype(F32)
        gate += partial[part, block:, :].astype(F32)
    hidden_grad[...] = total.astype(BF16)
    gate_grad[...] = gate[0:1, :width]


def call(kernel, outs, *args):
    return pl.pallas_call(
        kernel,
        out_shape=[jax.ShapeDtypeStruct(shape, dtype) for shape, dtype in outs],
        in_specs=[pl.BlockSpec(memory_space=pltpu.VMEM)] * len(args),
        out_specs=[pl.BlockSpec(memory_space=pltpu.VMEM)] * len(outs),
        compiler_params=pltpu.CompilerParams(vmem_limit_bytes=40 * 1024 * 1024),
    )(*args)


def on_device(residual, route_ids, slot_hidden, slot_gates, down_weight, cotangent):
    tokens, width = residual.shape
    experts, parts = lax.axis_size("expert"), lax.axis_size("tensor")
    slots, inner = slot_hidden.shape
    per = slots // experts
    weight = down_weight[0]
    gates = slot_gates[None, :]

    def bind(kernel, *sizes):
        return lambda *refs: kernel(*sizes, *refs)

    message, take, projected = call(
        bind(send_kernel, experts, per),
        [((2 * slots, width), BF16), ((2 * slots, tokens), BF16), ((slots, width), F32)],
        route_ids.T, cotangent, slot_hidden, weight, gates,
    )
    arrived = lax.all_to_all(
        message.reshape(experts, 2 * per, width), "expert", split_axis=0, concat_axis=0, tiled=True
    ).reshape(2 * slots, width)
    scaled, partial = call(
        bind(hidden_kernel, experts, per, parts),
        [((slots, width), BF16), ((parts, inner // parts + EXTRA, slots), BF16)],
        arrived, weight, gates, projected,
    )
    partial = lax.all_to_all(partial, "tensor", split_axis=0, concat_axis=0, tiled=True)
    (weight_terms,) = call(weight_kernel, [((inner, width), BF16)], slot_hidden, scaled)
    weight_grad = lax.psum_scatter(weight_terms, "dp", scatter_dimension=0, tiled=True)
    (combined,) = call(combine_kernel, [((tokens, width), BF16)], arrived, take, residual)
    hidden_grad, gate_grad = call(
        bind(sum_kernel, parts), [((inner // parts, slots), BF16), ((1, slots // parts), F32)], partial
    )
    return combined, hidden_grad.T, gate_grad[0], weight_grad[None]


def solution(mesh):
    placed = (
        P(("dp", "expert"), "tensor"),
        P(("dp", "expert"), None),
        P(("dp", "expert"), None),
        P(("dp", "expert")),
        P("expert", None, "tensor"),
        P(("dp", "expert"), "tensor"),
    )
    return jax.shard_map(
        on_device,
        mesh=mesh,
        in_specs=placed,
        out_specs=(
            P(("dp", "expert"), "tensor"),
            P(("dp", "expert"), "tensor"),
            P(("dp", "expert", "tensor")),
            P("expert", "dp", "tensor"),
        ),
        check_vma=False,
    )
```

```python
import functools

import jax
import jax.numpy as jnp
from jax import lax
from jax.experimental import pallas as pl
from jax.experimental.pallas import tpu as pltpu
from jax.sharding import PartitionSpec as P

F32 = jnp.float32
BF16 = jnp.bfloat16
EXTRA = 16
NEAR = jax.ShapeDtypeStruct


def iota(shape, dim):
    return lax.broadcasted_iota(jnp.int32, shape, dim)


def column_of(row):
    n = row.shape[1]
    same = iota((n, n), 0) == iota((n, n), 1)
    return jnp.sum(jnp.where(same, jnp.broadcast_to(row, (n, n)), 0.0), axis=1, keepdims=True)


def one_hot(mask):
    return mask.astype(F32).astype(BF16)


def dot(a, b, over=((1,), (0,))):
    return lax.dot_general(a, b, (over, ((), ())), preferred_element_type=F32)


def fetch(sources, targets, sems):
    copies = [pltpu.make_async_copy(s, t, sems.at[i]) for i, (s, t) in enumerate(zip(sources, targets))]
    for copy in copies:
        copy.start()
    return copies


def row_slots(slots, per, answers):
    row, slot = iota((2 * slots, slots), 0), iota((2 * slots, slots), 1)
    return one_hot(slot // per * (2 * per) + per * answers + slot % per == row)


def slot_rows(slots, per, answers):
    slot, row = iota((slots, 2 * slots), 0), iota((slots, 2 * slots), 1)
    return one_hot(slot // per * (2 * per) + per * answers + slot % per == row)


def send_kernel(
    per, ids_at, cotangent_at, hidden_at, weight_at, gates_at,
    message, hits, projected, ids, cotangent, hidden, weight, gates, sems,
):
    steps, slots, step = hidden.shape
    sources, targets = [ids_at, cotangent_at, gates_at], [ids, cotangent, gates]
    for k in range(steps):
        sources += [hidden_at.at[:, k * step : (k + 1) * step], weight_at.at[k * step : (k + 1) * step, :]]
        targets += [hidden.at[k], weight.at[k]]
    copies = fetch(sources, targets, sems)
    tokens = ids.shape[1]
    slot = iota((slots, tokens), 0)
    earlier = one_hot(iota((tokens, tokens), 0) < iota((tokens, tokens), 1))
    copies[0].wait()
    named = jnp.logical_or(ids[0:1, :] == slot // per, ids[1:2, :] == slot // per)
    rank = dot(one_hot(named), earlier).astype(jnp.int32)
    table = one_hot(jnp.logical_and(named, rank == slot % per))
    hits[...] = table
    copies[1].wait()
    rows = dot(row_slots(slots, per, 0), dot(table, cotangent[...]).astype(BF16))
    answers = row_slots(slots, per, 1)
    copies[2].wait()
    gate = column_of(gates[...])
    product = None
    for k in range(steps):
        copies[3 + 2 * k].wait()
        copies[4 + 2 * k].wait()
        term = dot(hidden[k], weight[k])
        product = term if product is None else product + term
    projected[...] = product
    message[...] = (rows + dot(answers, (gate * product).astype(BF16))).astype(BF16)


def hidden_kernel(per, parts, arrived, weight, gates, projected, scaled, partial_at, partial, sems):
    slots = scaled.shape[0]
    gate = column_of(gates[...])
    slot_grad = dot(slot_rows(slots, per, 0), arrived[...])
    grown = (gate * slot_grad).astype(BF16)
    scaled[...] = grown
    block = weight.shape[0] // parts
    copies = []
    for part in range(parts):
        partial[part, :block, :] = dot(weight[part * block : (part + 1) * block, :], grown, ((1,), (1,))).astype(BF16)
        copies += fetch(
            [partial.at[part, pl.ds(0, block)]], [partial_at.at[part, pl.ds(0, block)]], sems.at[pl.ds(part, 1)]
        )
    terms = jnp.sum(slot_grad * projected[...], axis=1, keepdims=True).astype(BF16).astype(F32)
    width = slots // parts
    chosen = one_hot(iota((parts, slots), 1) // width == iota((parts, slots), 0))
    lanes = jnp.where(iota((slots, slots), 0) % width == iota((slots, slots), 1), terms, 0.0).astype(BF16)
    gate_rows = dot(chosen, lanes)
    for part in range(parts):
        tail = jnp.where(iota((EXTRA, slots), 0) == 0, gate_rows[part : part + 1, :], 0.0)
        partial[part, block:, :] = tail.astype(BF16)
    copies += fetch(
        [partial.at[:, pl.ds(block, EXTRA)]], [partial_at.at[:, pl.ds(block, EXTRA)]], sems.at[pl.ds(parts, 1)]
    )
    for copy in copies:
        copy.wait()


def columns_of(hidden, part):
    width = hidden.shape[1] // 2
    return hidden[:, pl.ds(pl.multiple_of(part * width, 128), width)]


def weight_give_kernel(hidden, scaled, out):
    part = 1 - lax.axis_index("dp")
    out[...] = dot(columns_of(hidden, part), scaled[...], ((0,), (0,))).astype(BF16)


def weight_keep_kernel(hidden, scaled, got, out):
    part = lax.axis_index("dp")
    out[...] = (dot(columns_of(hidden, part), scaled[...], ((0,), (0,))) + got[...].astype(F32)).astype(BF16)


def combine_kernel(per, arrived, hits, residual, out):
    answers = dot(slot_rows(hits.shape[0], per, 1), arrived[...]).astype(BF16)
    out[...] = (residual[...].astype(F32) + dot(hits[...], answers, ((0,), (0,)))).astype(BF16)


def sum_kernel(parts, partial, weight_grad_at, hidden_grad, gate_grad):
    block, width = hidden_grad.shape[0], gate_grad.shape[1]
    total = partial[0, :block, :].astype(F32)
    gate = partial[0, block:, :].astype(F32)
    for part in range(1, parts):
        total += partial[part, :block, :].astype(F32)
        gate += partial[part, block:, :].astype(F32)
    hidden_grad[...] = total.astype(BF16)
    gate_grad[...] = gate[0:1, :width]


def call(kernel, sizes, outs, *args, far=0, scratch=()):
    near = len(args) - far
    args = args[:near] + tuple(pltpu.with_memory_space_constraint(arg, pltpu.HBM) for arg in args[near:])
    return pl.pallas_call(
        functools.partial(kernel, *sizes),
        out_shape=outs,
        in_specs=[pl.BlockSpec(memory_space=pltpu.VMEM)] * near + [pl.BlockSpec(memory_space=pltpu.HBM)] * far,
        out_specs=[
            pl.BlockSpec(memory_space=pltpu.VMEM if isinstance(out, NEAR) else pltpu.HBM) for out in outs
        ],
        scratch_shapes=list(scratch),
        compiler_params=pltpu.CompilerParams(vmem_limit_bytes=40 * 1024 * 1024),
    )(*args)


def on_device(residual, route_ids, slot_hidden, slot_gates, down_weight, cotangent):
    tokens, width = residual.shape
    experts, parts = lax.axis_size("expert"), lax.axis_size("tensor")
    slots, inner = slot_hidden.shape
    per = slots // experts
    weight = down_weight[0]
    gates = slot_gates[None, :]
    steps = inner // 512
    step = inner // steps

    message, hits, projected = call(
        send_kernel, (per,),
        [NEAR((2 * slots, width), BF16), NEAR((slots, tokens), BF16), NEAR((slots, width), F32)],
        route_ids.T, cotangent, slot_hidden, weight, gates, far=5,
        scratch=[
            pltpu.VMEM((2, tokens), jnp.int32), pltpu.VMEM((tokens, width), BF16),
            pltpu.VMEM((steps, slots, step), BF16), pltpu.VMEM((steps, step, width), BF16),
            pltpu.VMEM((1, slots), F32), pltpu.SemaphoreType.DMA((2 * steps + 3,)),
        ],
    )
    arrived = lax.all_to_all(
        message.reshape(experts, 2 * per, width), "expert", split_axis=0, concat_axis=0, tiled=True
    ).reshape(2 * slots, width)
    scaled, partial = call(
        hidden_kernel, (per, parts),
        [NEAR((slots, width), BF16), pltpu.HBM((parts, inner // parts + EXTRA, slots), BF16)],
        arrived, weight, gates, projected,
        scratch=[
            pltpu.VMEM((parts, inner // parts + EXTRA, slots), BF16), pltpu.SemaphoreType.DMA((parts + 1,)),
        ],
    )
    partial = lax.all_to_all(partial, "tensor", split_axis=0, concat_axis=0, tiled=True)
    (weight_give,) = call(weight_give_kernel, (), [NEAR((inner // 2, width), BF16)], slot_hidden, scaled)
    weight_got = lax.ppermute(weight_give, "dp", [(0, 1), (1, 0)])
    (weight_grad,) = call(
        weight_keep_kernel, (), [NEAR((inner // 2, width), BF16)], slot_hidden, scaled, weight_got
    )
    (combined,) = call(combine_kernel, (per,), [NEAR((tokens, width), BF16)], arrived, hits, residual)
    hidden_grad, gate_grad = call(
        sum_kernel, (parts,), [NEAR((inner // parts, slots), BF16), NEAR((1, slots // parts), F32)],
        partial, weight_grad, far=1,
    )
    return combined, hidden_grad.T, gate_grad[0], weight_grad[None]


def solution(mesh):
    placed = (
        P(("dp", "expert"), "tensor"),
        P(("dp", "expert"), None),
        P(("dp", "expert"), None),
        P(("dp", "expert")),
        P("expert", None, "tensor"),
        P(("dp", "expert"), "tensor"),
    )
    return jax.shard_map(
        on_device,
        mesh=mesh,
        in_specs=placed,
        out_specs=(
            P(("dp", "expert"), "tensor"),
            P(("dp", "expert"), "tensor"),
            P(("dp", "expert", "tensor")),
            P("expert", "dp", "tensor"),
        ),
        check_vma=False,
    )
```

```python
import functools

import jax
import jax.numpy as jnp
from jax import lax
from jax.experimental import pallas as pl
from jax.experimental.pallas import tpu as pltpu
from jax.sharding import PartitionSpec as P

F32 = jnp.float32
BF16 = jnp.bfloat16
EXTRA = 16
NEAR = jax.ShapeDtypeStruct


def iota(shape, dim):
    return lax.broadcasted_iota(jnp.int32, shape, dim)


def column_of(row):
    n = row.shape[1]
    same = iota((n, n), 0) == iota((n, n), 1)
    return jnp.sum(jnp.where(same, jnp.broadcast_to(row, (n, n)), 0.0), axis=1, keepdims=True)


def one_hot(mask):
    return mask.astype(F32).astype(BF16)


def dot(a, b, over=((1,), (0,))):
    return lax.dot_general(a, b, (over, ((), ())), preferred_element_type=F32)


def fetch(sources, targets, sems):
    copies = [pltpu.make_async_copy(s, t, sems.at[i]) for i, (s, t) in enumerate(zip(sources, targets))]
    for copy in copies:
        copy.start()
    return copies


def row_slots(slots, per, answers):
    row, slot = iota((2 * slots, slots), 0), iota((2 * slots, slots), 1)
    return one_hot(slot // per * (2 * per) + per * answers + slot % per == row)


def slot_rows(slots, per, answers):
    slot, row = iota((slots, 2 * slots), 0), iota((slots, 2 * slots), 1)
    return one_hot(slot // per * (2 * per) + per * answers + slot % per == row)


def send_kernel(
    per, step, ids_at, cotangent_at, hidden_at, weight_at, gates_at,
    message, hits, projected, hidden, weight, ids, cotangent, gates, sems,
):
    slots, inner = hidden.shape
    sources, targets = [ids_at, cotangent_at, gates_at], [ids, cotangent, gates]
    spans = [pl.ds(begin, step) for begin in range(0, inner, step)]
    for span in spans:
        sources += [hidden_at.at[:, span], weight_at.at[span]]
        targets += [hidden.at[:, span], weight.at[span]]
    copies = fetch(sources, targets, sems)
    tokens = ids.shape[1]
    slot = iota((slots, tokens), 0)
    earlier = one_hot(iota((tokens, tokens), 0) < iota((tokens, tokens), 1))
    copies[0].wait()
    named = jnp.logical_or(ids[0:1, :] == slot // per, ids[1:2, :] == slot // per)
    rank = dot(one_hot(named), earlier).astype(jnp.int32)
    table = one_hot(jnp.logical_and(named, rank == slot % per))
    hits[...] = table
    copies[1].wait()
    rows = dot(row_slots(slots, per, 0), dot(table, cotangent[...]).astype(BF16))
    answers = row_slots(slots, per, 1)
    copies[2].wait()
    gate = column_of(gates[...])
    product = None
    for k, span in enumerate(spans):
        copies[3 + 2 * k].wait()
        copies[4 + 2 * k].wait()
        term = dot(hidden[:, span], weight[span, :])
        product = term if product is None else product + term
    projected[...] = product
    message[...] = (rows + dot(answers, (gate * product).astype(BF16))).astype(BF16)


def hidden_kernel(per, parts, arrived, weight, gates, projected, scaled, partial_at, partial, sems):
    slots = scaled.shape[0]
    gate = column_of(gates[...])
    slot_grad = dot(slot_rows(slots, per, 0), arrived[...])
    grown = (gate * slot_grad).astype(BF16)
    scaled[...] = grown
    terms = jnp.sum(slot_grad * projected[...], axis=1, keepdims=True).astype(BF16).astype(F32)
    width = slots // parts
    chosen = one_hot(iota((parts, slots), 1) // width == iota((parts, slots), 0))
    lanes = jnp.where(iota((slots, slots), 0) % width == iota((slots, slots), 1), terms, 0.0).astype(BF16)
    gate_rows = dot(chosen, lanes)
    block = weight.shape[0] // parts
    copies = []
    for part in range(parts):
        tail = jnp.where(iota((EXTRA, slots), 0) == 0, gate_rows[part : part + 1, :], 0.0)
        partial[part, block:, :] = tail.astype(BF16)
        partial[part, :block, :] = dot(weight[part * block : (part + 1) * block, :], grown, ((1,), (1,))).astype(BF16)
        copies += fetch([partial.at[part]], [partial_at.at[part]], sems.at[pl.ds(part, 1)])
    for copy in copies:
        copy.wait()


def columns_of(hidden, part):
    width = hidden.shape[1] // 2
    return hidden[:, pl.ds(pl.multiple_of(part * width, 128), width)]


def weight_give_kernel(hidden, scaled, first, second):
    product = dot(columns_of(hidden, 1 - lax.axis_index("dp")), scaled[...], ((0,), (0,))).astype(BF16)
    half = first.shape[0]
    first[...] = product[:half]
    second[...] = product[half:]


def weight_keep_kernel(hidden, scaled, first, second, out):
    product = dot(columns_of(hidden, lax.axis_index("dp")), scaled[...], ((0,), (0,)))
    half = first.shape[0]
    out[:half, :] = (product[:half] + first[...].astype(F32)).astype(BF16)
    out[half:, :] = (product[half:] + second[...].astype(F32)).astype(BF16)


def combine_kernel(per, arrived, hits, residual, out):
    answers = dot(slot_rows(hits.shape[0], per, 1), arrived[...]).astype(BF16)
    out[...] = (residual[...].astype(F32) + dot(hits[...], answers, ((0,), (0,)))).astype(BF16)


def sum_kernel(parts, partial, weight_grad_at, hidden_grad, gate_grad):
    block, width = hidden_grad.shape[0], gate_grad.shape[1]
    total = partial[0, :block, :].astype(F32)
    gate = partial[0, block:, :].astype(F32)
    for part in range(1, parts):
        total += partial[part, :block, :].astype(F32)
        gate += partial[part, block:, :].astype(F32)
    hidden_grad[...] = total.astype(BF16)
    gate_grad[...] = gate[0:1, :width]


def call(kernel, sizes, outs, *args, far=0, scratch=()):
    near = len(args) - far
    args = args[:near] + tuple(pltpu.with_memory_space_constraint(arg, pltpu.HBM) for arg in args[near:])
    return pl.pallas_call(
        functools.partial(kernel, *sizes),
        out_shape=outs,
        in_specs=[pl.BlockSpec(memory_space=pltpu.VMEM)] * near + [pl.BlockSpec(memory_space=pltpu.HBM)] * far,
        out_specs=[
            pl.BlockSpec(memory_space=pltpu.VMEM if isinstance(out, NEAR) else out.memory_space) for out in outs
        ],
        scratch_shapes=list(scratch),
        compiler_params=pltpu.CompilerParams(vmem_limit_bytes=40 * 1024 * 1024),
    )(*args)


def on_device(residual, route_ids, slot_hidden, slot_gates, down_weight, cotangent):
    tokens, width = residual.shape
    experts, parts = lax.axis_size("expert"), lax.axis_size("tensor")
    slots, inner = slot_hidden.shape
    per = slots // experts
    gates = slot_gates[None, :]
    step = 512

    message, hits, projected, hidden, weight = call(
        send_kernel, (per, step),
        [
            NEAR((2 * slots, width), BF16), NEAR((slots, tokens), BF16), NEAR((slots, width), F32),
            pltpu.VMEM((slots, inner), BF16), pltpu.VMEM((inner, width), BF16),
        ],
        route_ids.T, cotangent, slot_hidden, down_weight[0], gates, far=5,
        scratch=[
            pltpu.VMEM((2, tokens), jnp.int32), pltpu.VMEM((tokens, width), BF16),
            pltpu.VMEM((1, slots), F32), pltpu.SemaphoreType.DMA((2 * (inner // step) + 3,)),
        ],
    )
    arrived = lax.all_to_all(
        message.reshape(experts, 2 * per, width), "expert", split_axis=0, concat_axis=0, tiled=True
    ).reshape(2 * slots, width)
    scaled, partial = call(
        hidden_kernel, (per, parts),
        [NEAR((slots, width), BF16), pltpu.HBM((parts, inner // parts + EXTRA, slots), BF16)],
        arrived, weight, gates, projected,
        scratch=[
            pltpu.VMEM((parts, inner // parts + EXTRA, slots), BF16), pltpu.SemaphoreType.DMA((parts,)),
        ],
    )
    partial = lax.all_to_all(partial, "tensor", split_axis=0, concat_axis=0, tiled=True)
    weight_give = call(weight_give_kernel, (), [NEAR((inner // 4, width), BF16)] * 2, hidden, scaled)
    weight_got = [lax.ppermute(part, "dp", [(0, 1), (1, 0)]) for part in weight_give]
    (weight_grad,) = call(
        weight_keep_kernel, (), [NEAR((inner // 2, width), BF16)], hidden, scaled, *weight_got
    )
    (combined,) = call(combine_kernel, (per,), [NEAR((tokens, width), BF16)], arrived, hits, residual)
    hidden_grad, gate_grad = call(
        sum_kernel, (parts,), [NEAR((inner // parts, slots), BF16), NEAR((1, slots // parts), F32)],
        partial, weight_grad, far=1,
    )
    return combined, hidden_grad.T, gate_grad[0], weight_grad[None]


def solution(mesh):
    placed = (
        P(("dp", "expert"), "tensor"),
        P(("dp", "expert"), None),
        P(("dp", "expert"), None),
        P(("dp", "expert")),
        P("expert", None, "tensor"),
        P(("dp", "expert"), "tensor"),
    )
    return jax.shard_map(
        on_device,
        mesh=mesh,
        in_specs=placed,
        out_specs=(
            P(("dp", "expert"), "tensor"),
            P(("dp", "expert"), "tensor"),
            P(("dp", "expert", "tensor")),
            P("expert", "dp", "tensor"),
        ),
        check_vma=False,
    )
```

```python
import functools

import jax
import jax.numpy as jnp
from jax import lax
from jax.experimental import pallas as pl
from jax.experimental.pallas import tpu as pltpu
from jax.sharding import PartitionSpec as P

F32 = jnp.float32
BF16 = jnp.bfloat16
EXTRA = 16
NEAR = jax.ShapeDtypeStruct


def iota(shape, dim):
    return lax.broadcasted_iota(jnp.int32, shape, dim)


def column_of(row):
    n = row.shape[1]
    same = iota((n, n), 0) == iota((n, n), 1)
    return jnp.sum(jnp.where(same, jnp.broadcast_to(row, (n, n)), 0.0), axis=1, keepdims=True)


def one_hot(mask):
    return mask.astype(F32).astype(BF16)


def dot(a, b, over=((1,), (0,))):
    return lax.dot_general(a, b, (over, ((), ())), preferred_element_type=F32)


def fetch(sources, targets, sems):
    copies = [pltpu.make_async_copy(s, t, sems.at[i]) for i, (s, t) in enumerate(zip(sources, targets))]
    for copy in copies:
        copy.start()
    return copies


def row_slots(slots, per, answers):
    row, slot = iota((2 * slots, slots), 0), iota((2 * slots, slots), 1)
    return one_hot(slot // per * (2 * per) + per * answers + slot % per == row)


def slot_rows(slots, per, answers):
    slot, row = iota((slots, 2 * slots), 0), iota((slots, 2 * slots), 1)
    return one_hot(slot // per * (2 * per) + per * answers + slot % per == row)


def send_kernel(
    per, step, token, ids_at, cotangent_at, hidden_at, weight_at, gates_at,
    message, hits, projected, hidden, weight, ids, cotangent, gates, sems,
):
    slots, inner = hidden.shape
    sources, targets = [ids_at, cotangent_at, gates_at], [ids, cotangent, gates]
    spans = [pl.ds(begin, step) for begin in range(0, inner, step)]
    for span in spans:
        sources += [hidden_at.at[:, span], weight_at.at[span]]
        targets += [hidden.at[:, span], weight.at[span]]
    copies = fetch(sources, targets, sems)
    tokens = ids.shape[1]
    slot = iota((slots, tokens), 0)
    earlier = one_hot(iota((tokens, tokens), 0) < iota((tokens, tokens), 1))
    copies[0].wait()
    named = jnp.logical_or(ids[0:1, :] == slot // per, ids[1:2, :] == slot // per)
    rank = dot(one_hot(named), earlier).astype(jnp.int32)
    table = one_hot(jnp.logical_and(named, rank == slot % per))
    hits[...] = table
    copies[1].wait()
    rows = dot(row_slots(slots, per, 0), dot(table, cotangent[...]).astype(BF16))
    answers = row_slots(slots, per, 1)
    copies[2].wait()
    gate = column_of(gates[...])
    product = None
    for k, span in enumerate(spans):
        copies[3 + 2 * k].wait()
        copies[4 + 2 * k].wait()
        term = dot(hidden[:, span], weight[span, :])
        product = term if product is None else product + term
    projected[...] = product
    message[...] = (rows + dot(answers, (gate * product).astype(BF16))).astype(BF16)


def hidden_kernel(per, parts, arrived, weight, gates, projected, scaled, partial_at, partial, sems):
    slots = scaled.shape[0]
    gate = column_of(gates[...])
    slot_grad = dot(slot_rows(slots, per, 0), arrived[...])
    grown = (gate * slot_grad).astype(BF16)
    scaled[...] = grown
    block = weight.shape[0] // parts
    copies = []
    for part in range(parts):
        partial[part, :block, :] = dot(weight[part * block : (part + 1) * block, :], grown, ((1,), (1,))).astype(BF16)
        span = part, pl.ds(0, block)
        copies += fetch([partial.at[span]], [partial_at.at[span]], sems.at[pl.ds(part, 1)])
    terms = jnp.sum(slot_grad * projected[...], axis=1, keepdims=True).astype(BF16).astype(F32)
    width = slots // parts
    chosen = one_hot(iota((parts, slots), 1) // width == iota((parts, slots), 0))
    lanes = jnp.where(iota((slots, slots), 0) % width == iota((slots, slots), 1), terms, 0.0).astype(BF16)
    gate_rows = dot(chosen, lanes)
    for part in range(parts):
        tail = jnp.where(iota((EXTRA, slots), 0) == 0, gate_rows[part : part + 1, :], 0.0)
        partial[part, block:, :] = tail.astype(BF16)
    span = slice(None), pl.ds(block, EXTRA)
    copies += fetch([partial.at[span]], [partial_at.at[span]], sems.at[pl.ds(parts, 1)])
    for copy in copies:
        copy.wait()


def columns_of(hidden, part):
    width = hidden.shape[1] // 2
    return hidden[:, pl.ds(pl.multiple_of(part * width, 128), width)]


def weight_give_kernel(hidden, scaled, first, second):
    product = dot(columns_of(hidden, 1 - lax.axis_index("dp")), scaled[...], ((0,), (0,))).astype(BF16)
    half = first.shape[0]
    first[...] = product[:half]
    second[...] = product[half:]


def weight_keep_kernel(hidden, scaled, first, second, out):
    product = dot(columns_of(hidden, lax.axis_index("dp")), scaled[...], ((0,), (0,)))
    half = first.shape[0]
    out[:half, :] = (product[:half] + first[...].astype(F32)).astype(BF16)
    out[half:, :] = (product[half:] + second[...].astype(F32)).astype(BF16)


def combine_kernel(per, arrived, hits, residual, out):
    answers = dot(slot_rows(hits.shape[0], per, 1), arrived[...]).astype(BF16)
    out[...] = (residual[...].astype(F32) + dot(hits[...], answers, ((0,), (0,)))).astype(BF16)


def sum_kernel(parts, partial, weight_grad_at, hidden_grad, gate_grad):
    block, width = hidden_grad.shape[0], gate_grad.shape[1]
    total = partial[0, :block, :].astype(F32)
    gate = partial[0, block:, :].astype(F32)
    for part in range(1, parts):
        total += partial[part, :block, :].astype(F32)
        gate += partial[part, block:, :].astype(F32)
    hidden_grad[...] = total.astype(BF16)
    gate_grad[...] = gate[0:1, :width]


def call(kernel, sizes, outs, *args, far=0, scratch=()):
    near = len(args) - far
    args = args[:near] + tuple(pltpu.with_memory_space_constraint(arg, pltpu.HBM) for arg in args[near:])
    return pl.pallas_call(
        functools.partial(kernel, *sizes),
        out_shape=outs,
        in_specs=[pl.BlockSpec(memory_space=pltpu.VMEM)] * near + [pl.BlockSpec(memory_space=pltpu.HBM)] * far,
        out_specs=[
            pl.BlockSpec(memory_space=pltpu.VMEM if isinstance(out, NEAR) else out.memory_space) for out in outs
        ],
        scratch_shapes=list(scratch),
        compiler_params=pltpu.CompilerParams(vmem_limit_bytes=40 * 1024 * 1024),
    )(*args)


def on_device(residual, route_ids, slot_hidden, slot_gates, down_weight, cotangent):
    tokens, width = residual.shape
    experts, parts = lax.axis_size("expert"), lax.axis_size("tensor")
    slots, inner = slot_hidden.shape
    per = slots // experts
    gates = slot_gates[None, :]
    step = 512

    token = lax.ppermute(
        gates, ("dp", "expert"), [(experts + i, experts + (i + experts // 4) % experts) for i in range(experts)]
    )
    message, hits, projected, hidden, weight = call(
        send_kernel, (per, step),
        [
            NEAR((2 * slots, width), BF16), NEAR((slots, tokens), BF16), NEAR((slots, width), F32),
            pltpu.VMEM((slots, inner), BF16), pltpu.VMEM((inner, width), BF16),
        ],
        token, route_ids.T, cotangent, slot_hidden, down_weight[0], gates, far=5,
        scratch=[
            pltpu.VMEM((2, tokens), jnp.int32), pltpu.VMEM((tokens, width), BF16),
            pltpu.VMEM((1, slots), F32), pltpu.SemaphoreType.DMA((2 * (inner // step) + 3,)),
        ],
    )
    arrived = lax.all_to_all(
        message.reshape(experts, 2 * per, width), "expert", split_axis=0, concat_axis=0, tiled=True
    ).reshape(2 * slots, width)
    scaled, partial = call(
        hidden_kernel, (per, parts),
        [NEAR((slots, width), BF16), pltpu.HBM((parts, inner // parts + EXTRA, slots), BF16)],
        arrived, weight, gates, projected,
        scratch=[
            pltpu.VMEM((parts, inner // parts + EXTRA, slots), BF16), pltpu.SemaphoreType.DMA((parts + 1,)),
        ],
    )
    partial = lax.all_to_all(partial, "tensor", split_axis=0, concat_axis=0, tiled=True)
    weight_give = call(weight_give_kernel, (), [NEAR((inner // 4, width), BF16)] * 2, hidden, scaled)
    weight_got = [lax.ppermute(part, "dp", [(0, 1), (1, 0)]) for part in weight_give]
    (weight_grad,) = call(
        weight_keep_kernel, (), [NEAR((inner // 2, width), BF16)], hidden, scaled, *weight_got
    )
    (combined,) = call(combine_kernel, (per,), [NEAR((tokens, width), BF16)], arrived, hits, residual)
    hidden_grad, gate_grad = call(
        sum_kernel, (parts,), [NEAR((inner // parts, slots), BF16), NEAR((1, slots // parts), F32)],
        partial, weight_grad, far=1,
    )
    return combined, hidden_grad.T, gate_grad[0], weight_grad[None]


def solution(mesh):
    placed = (
        P(("dp", "expert"), "tensor"),
        P(("dp", "expert"), None),
        P(("dp", "expert"), None),
        P(("dp", "expert")),
        P("expert", None, "tensor"),
        P(("dp", "expert"), "tensor"),
    )
    return jax.shard_map(
        on_device,
        mesh=mesh,
        in_specs=placed,
        out_specs=(
            P(("dp", "expert"), "tensor"),
            P(("dp", "expert"), "tensor"),
            P(("dp", "expert", "tensor")),
            P("expert", "dp", "tensor"),
        ),
        check_vma=False,
    )
```

```python
import functools

import jax
import jax.numpy as jnp
from jax import lax
from jax.experimental import pallas as pl
from jax.experimental.pallas import tpu as pltpu
from jax.sharding import PartitionSpec as P

F32 = jnp.float32
BF16 = jnp.bfloat16
EXTRA = 16
NEAR = jax.ShapeDtypeStruct


def iota(shape, dim):
    return lax.broadcasted_iota(jnp.int32, shape, dim)


def column_of(row):
    n = row.shape[1]
    same = iota((n, n), 0) == iota((n, n), 1)
    return jnp.sum(jnp.where(same, jnp.broadcast_to(row, (n, n)), 0.0), axis=1, keepdims=True)


def one_hot(mask):
    return mask.astype(F32).astype(BF16)


def dot(a, b, over=((1,), (0,))):
    return lax.dot_general(a, b, (over, ((), ())), preferred_element_type=F32)


def fetch(sources, targets, sems):
    copies = [pltpu.make_async_copy(s, t, sems.at[i]) for i, (s, t) in enumerate(zip(sources, targets))]
    for copy in copies:
        copy.start()
    return copies


def pairs_of(rows):
    tiles = rows.reshape(-1, 2, 8, rows.shape[1])
    return tiles[:, 0], tiles[:, 1]


def interleave(picks, answers):
    picks, answers = (x.reshape(-1, 8, x.shape[1]) for x in (picks, answers))
    low = lax.broadcasted_iota(jnp.int32, picks.shape, 1) < 4
    even = jnp.where(low, picks, pltpu.roll(answers, 4, 1))
    odd = jnp.where(low, pltpu.roll(picks, 4, 1), answers)
    return jnp.stack([even, odd], axis=1).reshape(-1, picks.shape[2])


def picks_of(rows):
    even, odd = pairs_of(rows)
    low = lax.broadcasted_iota(jnp.int32, even.shape, 1) < 4
    return jnp.where(low, even, pltpu.roll(odd, 4, 1)).reshape(-1, rows.shape[1])


def slot_rows(slots, per, answers):
    slot, row = iota((slots, 2 * slots), 0), iota((slots, 2 * slots), 1)
    return one_hot(slot // per * (2 * per) + per * answers + slot % per == row)


def send_kernel(
    per, step, token, ids_at, cotangent_at, hidden_at, weight_at, gates_at,
    message, hits, projected, hidden, weight, ids, cotangent, gates, sems,
):
    slots, inner = hidden.shape
    sources, targets = [ids_at, cotangent_at, gates_at], [ids, cotangent, gates]
    spans = [pl.ds(begin, step) for begin in range(0, inner, step)]
    for span in spans:
        sources += [hidden_at.at[:, span], weight_at.at[span]]
        targets += [hidden.at[:, span], weight.at[span]]
    copies = fetch(sources, targets, sems)
    tokens = ids.shape[1]
    slot = iota((slots, tokens), 0)
    earlier = one_hot(iota((tokens, tokens), 0) < iota((tokens, tokens), 1))
    copies[0].wait()
    named = jnp.logical_or(ids[0:1, :] == slot // per, ids[1:2, :] == slot // per)
    rank = dot(one_hot(named), earlier).astype(jnp.int32)
    table = one_hot(jnp.logical_and(named, rank == slot % per))
    hits[...] = table
    copies[1].wait()
    picks = dot(table, cotangent[...])
    copies[2].wait()
    gate = column_of(gates[...])
    product = None
    for k, span in enumerate(spans):
        copies[3 + 2 * k].wait()
        copies[4 + 2 * k].wait()
        term = dot(hidden[:, span], weight[span, :])
        product = term if product is None else product + term
    projected[...] = product
    message[...] = interleave(picks, gate * product).astype(BF16)


def hidden_kernel(per, parts, arrived, weight, gates, projected, scaled, partial_at, partial, sems):
    slots = scaled.shape[0]
    gate = column_of(gates[...])
    slot_grad = picks_of(arrived[...].astype(F32))
    grown = (gate * slot_grad).astype(BF16)
    scaled[...] = grown
    block = weight.shape[0] // parts
    copies = []
    for part in range(parts):
        partial[part, :block, :] = dot(weight[part * block : (part + 1) * block, :], grown, ((1,), (1,))).astype(BF16)
        span = part, pl.ds(0, block)
        copies += fetch([partial.at[span]], [partial_at.at[span]], sems.at[pl.ds(part, 1)])
        if part == parts // 2 - 1:
            terms = jnp.sum(slot_grad * projected[...], axis=1, keepdims=True).astype(BF16).astype(F32)
            width = slots // parts
            chosen = one_hot(iota((parts, slots), 1) // width == iota((parts, slots), 0))
            lanes = jnp.where(iota((slots, slots), 0) % width == iota((slots, slots), 1), terms, 0.0).astype(BF16)
            gate_rows = dot(chosen, lanes)
            for at in range(parts):
                tail = jnp.where(iota((EXTRA, slots), 0) == 0, gate_rows[at : at + 1, :], 0.0)
                partial[at, block:, :] = tail.astype(BF16)
            span = slice(None), pl.ds(block, EXTRA)
            copies += fetch([partial.at[span]], [partial_at.at[span]], sems.at[pl.ds(parts, 1)])
    for copy in copies:
        copy.wait()


def columns_of(hidden, part):
    width = hidden.shape[1] // 2
    return hidden[:, pl.ds(pl.multiple_of(part * width, 128), width)]


def weight_give_kernel(hidden, scaled, first, second):
    product = dot(columns_of(hidden, 1 - lax.axis_index("dp")), scaled[...], ((0,), (0,))).astype(BF16)
    half = first.shape[0]
    first[...] = product[:half]
    second[...] = product[half:]


def weight_keep_kernel(hidden, scaled, first, second, out):
    product = dot(columns_of(hidden, lax.axis_index("dp")), scaled[...], ((0,), (0,)))
    half = first.shape[0]
    out[:half, :] = (product[:half] + first[...].astype(F32)).astype(BF16)
    out[half:, :] = (product[half:] + second[...].astype(F32)).astype(BF16)


def combine_kernel(per, arrived, hits, residual, out):
    answers = dot(slot_rows(hits.shape[0], per, 1), arrived[...]).astype(BF16)
    out[...] = (residual[...].astype(F32) + dot(hits[...], answers, ((0,), (0,)))).astype(BF16)


def sum_kernel(parts, partial, weight_grad_at, hidden_grad, gate_grad):
    block, width = hidden_grad.shape[0], gate_grad.shape[1]
    total = partial[0, :block, :].astype(F32)
    gate = partial[0, block:, :].astype(F32)
    for part in range(1, parts):
        total += partial[part, :block, :].astype(F32)
        gate += partial[part, block:, :].astype(F32)
    hidden_grad[...] = total.astype(BF16)
    gate_grad[...] = gate[0:1, :width]


def call(kernel, sizes, outs, *args, far=0, scratch=()):
    near = len(args) - far
    args = args[:near] + tuple(pltpu.with_memory_space_constraint(arg, pltpu.HBM) for arg in args[near:])
    return pl.pallas_call(
        functools.partial(kernel, *sizes),
        out_shape=outs,
        in_specs=[pl.BlockSpec(memory_space=pltpu.VMEM)] * near + [pl.BlockSpec(memory_space=pltpu.HBM)] * far,
        out_specs=[
            pl.BlockSpec(memory_space=pltpu.VMEM if isinstance(out, NEAR) else out.memory_space) for out in outs
        ],
        scratch_shapes=list(scratch),
        compiler_params=pltpu.CompilerParams(vmem_limit_bytes=40 * 1024 * 1024),
    )(*args)


def on_device(residual, route_ids, slot_hidden, slot_gates, down_weight, cotangent):
    tokens, width = residual.shape
    experts, parts = lax.axis_size("expert"), lax.axis_size("tensor")
    slots, inner = slot_hidden.shape
    per = slots // experts
    gates = slot_gates[None, :]
    step = 512

    token = lax.ppermute(
        gates, ("dp", "expert"), [(experts + i, experts + (i + experts // 4) % experts) for i in range(experts)]
    )
    message, hits, projected, hidden, weight = call(
        send_kernel, (per, step),
        [
            NEAR((2 * slots, width), BF16), NEAR((slots, tokens), BF16), NEAR((slots, width), F32),
            pltpu.VMEM((slots, inner), BF16), pltpu.VMEM((inner, width), BF16),
        ],
        token, route_ids.T, cotangent, slot_hidden, down_weight[0], gates, far=5,
        scratch=[
            pltpu.VMEM((2, tokens), jnp.int32), pltpu.VMEM((tokens, width), BF16),
            pltpu.VMEM((1, slots), F32), pltpu.SemaphoreType.DMA((2 * (inner // step) + 3,)),
        ],
    )
    arrived = lax.all_to_all(
        message.reshape(experts, 2 * per, width), "expert", split_axis=0, concat_axis=0, tiled=True
    ).reshape(2 * slots, width)
    scaled, partial = call(
        hidden_kernel, (per, parts),
        [NEAR((slots, width), BF16), pltpu.HBM((parts, inner // parts + EXTRA, slots), BF16)],
        arrived, weight, gates, projected,
        scratch=[
            pltpu.VMEM((parts, inner // parts + EXTRA, slots), BF16), pltpu.SemaphoreType.DMA((parts + 1,)),
        ],
    )
    partial = lax.all_to_all(partial, "tensor", split_axis=0, concat_axis=0, tiled=True)
    weight_give = call(weight_give_kernel, (), [NEAR((inner // 4, width), BF16)] * 2, hidden, scaled)
    weight_got = [lax.ppermute(part, "dp", [(0, 1), (1, 0)]) for part in weight_give]
    (weight_grad,) = call(
        weight_keep_kernel, (), [NEAR((inner // 2, width), BF16)], hidden, scaled, *weight_got
    )
    (combined,) = call(combine_kernel, (per,), [NEAR((tokens, width), BF16)], arrived, hits, residual)
    hidden_grad, gate_grad = call(
        sum_kernel, (parts,), [NEAR((inner // parts, slots), BF16), NEAR((1, slots // parts), F32)],
        partial, weight_grad, far=1,
    )
    return combined, hidden_grad.T, gate_grad[0], weight_grad[None]


def solution(mesh):
    placed = (
        P(("dp", "expert"), "tensor"),
        P(("dp", "expert"), None),
        P(("dp", "expert"), None),
        P(("dp", "expert")),
        P("expert", None, "tensor"),
        P(("dp", "expert"), "tensor"),
    )
    return jax.shard_map(
        on_device,
        mesh=mesh,
        in_specs=placed,
        out_specs=(
            P(("dp", "expert"), "tensor"),
            P(("dp", "expert"), "tensor"),
            P(("dp", "expert", "tensor")),
            P("expert", "dp", "tensor"),
        ),
        check_vma=False,
    )
```
